32 devices in a mesh: groups: 2 (over x), gz: 16 (over z, y, core).
Axes of the slice: x: 2, y: 2, z: 4, core: 2. Of those that a mesh axis runs over, the one named last changes fastest.
Arguments:
- positions: float32 [32, 2, 4096], P(('groups', 'gz')), parts along dimension 0, may hold values from -6 to 6
- edges: int32 [32, 2, 8192], P(('groups', 'gz')), parts along dimension 0, may hold values from 0 to 4095
- rest_length: float32 [32, 8192], P(('groups', 'gz')), parts along dimension 0, may hold values from 0.5 to 2
- stiffness: float32 [32, 8192], P(('groups', 'gz')), parts along dimension 0, may hold values from 0.5 to 18, as said below
- corr_index: int32 [32, 2, 1024], P(('groups', 'gz')), parts along dimension 0, may hold values from 0 to 4095
- corr_count: int32 [32], P(('groups', 'gz')), parts along dimension 0, may hold values from 0 to 1024, as said below
- fixed: int32 [32], P(('groups', 'gz')), parts along dimension 0, may hold values 0 or 1
Outputs:
- solution_field: float32 [32, 2, 4096], P(('groups', 'gz')), parts along dimension 0
- residual: float32 [32, 2, 4096], P(('groups', 'gz')), parts along dimension 0
The draws below stay inside these ranges and needn't reach their ends.
There are 2 independent parts, one for each index of `groups`. The reference program is written for one: setup_inputs(seed, part) draws one part's arguments, and reference() takes and returns one part's arrays. A program takes and returns all parts, laid end to end along the dimension named above; each array names one. Nothing has to cross between parts.
Inputs may be any that keep to these rules, and one draw needn't show every extreme that they name: `stiffness`: sections further down the slab tend to be stiffer. `corr_count`: the last pair has count 0; in every draw one pair has exactly 1024 live slots. `corr_index`: slots at or past a pair's count carry no correspondence.
All inputs are finite; a program needn't handle non-finite values. No bound on the sum of `fixed` on one device may be relied on, other than what follows from the above.
Results may differ from the reference program's by a relative error of at most 0.00015.
Values sent between devices are 32-bit elements; how exact they have to be, the bound alone decides.
A program may use at most 64 MiB of HBM per device.

```python
import math
import jax
import jax.numpy as jnp
from jax import lax

V = 4096
E = 8192
C = 1024
ITERS = 4
SECTIONS = 16


def draw_stiffness(key, part):
    key = jax.random.fold_in(key, 7)
    first = jax.random.fold_in(key, 0)
    ramp_scale = 1.0 + 2.0 * jnp.arange(SECTIONS, dtype=jnp.float32)[:, None] / (SECTIONS - 1)
    base_draw = jnp.exp(jax.random.uniform(first, (SECTIONS, E), jnp.float32, math.log(0.5), math.log(2.0)))
    return (base_draw * ramp_scale).astype(jnp.float32)


def draw_corr_count(key, part):
    key = jax.random.fold_in(key, 11)
    first, second = jax.random.split(key)
    counts = jax.random.randint(first, (SECTIONS,), C // 3, C + 1)
    full_at = jax.random.randint(second, (), 0, SECTIONS - 1)
    places = jnp.arange(SECTIONS)
    counts = jnp.where(places == full_at, C, counts)
    counts = jnp.where(places == SECTIONS - 1, 0, counts)
    return counts.astype(jnp.int32)


def place_ends(array, stream_key, least, top_value):
    longest = array.shape.index(max(array.shape))
    spots = []
    for shift in (0, 1):
        where = [jax.random.randint(jax.random.fold_in(stream_key, axis), (), 0, length) for axis, length in enumerate(array.shape)]
        where[longest] = (where[longest] + shift) % array.shape[longest]
        spots.append(tuple(where))
    return array.at[spots[0]].set(least).at[spots[1]].set(top_value)


def steps_of(rng, dims, cuts, smallest, largest):
    factor_of = 1.0
    for dim, parts in cuts:
        draws = jax.random.uniform(jax.random.fold_in(jax.random.fold_in(rng, 6), dim), (parts,), jnp.float32, smallest / len(cuts), largest / len(cuts))
        factor_of = factor_of * jnp.repeat(jnp.exp(draws), dims[dim] // parts).reshape((-1,) + (1,) * (len(dims) - 1 - dim))
    return factor_of


def normal_values(key, extent, scale, limit, cuts=(), kind=jnp.bfloat16):
    array = jax.random.normal(key, extent, jnp.float32) * scale
    if len(cuts) > 0:
        array = steps_of(key, extent, cuts, -0.22, 0.18) * array
    return jnp.clip(array, min=-limit, max=limit).astype(kind)


def setup_inputs(seed: int = 0, part: int = 0) -> dict:
    key_of = jax.random.split(jax.random.key(seed), 8)
    own_keys = jax.random.split(jax.random.fold_in(key_of[7], part), 8)
    positions = normal_values(own_keys[0], (SECTIONS, 2, V), 1.0, 6.0, ((0, 16),), jnp.float32)
    edges = place_ends(jax.random.randint(own_keys[1], (SECTIONS, 2, E), 0, V), jax.random.fold_in(own_keys[1], 1), 0, V - 1).astype(jnp.int32)
    rest_length = jnp.clip(jnp.exp(math.log(2.0) - 1.3862944 * jax.random.uniform(own_keys[2], (SECTIONS, E), jnp.float32) ** steps_of(own_keys[2], (SECTIONS, E), ((0, 16),), -0.2, 0.2)), 0.5, 2.0)
    stiffness = draw_stiffness(jax.random.fold_in(jax.random.fold_in(key_of[7], part), 71), part)
    corr_index = place_ends(jax.random.randint(own_keys[4], (SECTIONS, 2, C), 0, V), jax.random.fold_in(own_keys[4], 1), 0, V - 1).astype(jnp.int32)
    corr_count = draw_corr_count(jax.random.fold_in(jax.random.fold_in(key_of[7], part), 71), part)
    fixed = place_ends((jax.random.randint(own_keys[6], (SECTIONS,), 0, 4) < 1).astype(jnp.int32), jax.random.fold_in(own_keys[6], 1), 0, 1)
    return {"positions": positions, "edges": edges, "rest_length": rest_length, "stiffness": stiffness, "corr_index": corr_index, "corr_count": corr_count, "fixed": fixed}


DAMPING = 0.05

def spring_parts(points, edge_pair, rest, stiff):
    spread = points[:, edge_pair[0]] - points[:, edge_pair[1]]
    length = jnp.sqrt(lax.optimization_barrier(jnp.sum(spread * spread, axis=0)) + 1.0)
    return (stiff * (length - rest), stiff * spread / length)

def pick_rows(field, index):
    return field[:, index]

def add_rows(accum, index, values):
    return accum.at[:, index].add(values)

def reference(positions, edges, rest_length, stiffness, corr_index, corr_count, fixed):
    slots = lax.iota(jnp.int32, corr_index.shape[2])
    active = (slots[None, :] < corr_count[:, None]).astype(jnp.float32)[:, None, :]
    movable = (1 - fixed).astype(jnp.float32)[:, None, None]
    spring_res, slopes = jax.vmap(spring_parts)(positions, edges, rest_length, stiffness)
    near_idx = corr_index[:, 0]
    far_idx = corr_index[:, 1]
    head_idx = edges[:, 0]
    tail_idx = edges[:, 1]
    picker = jax.vmap(pick_rows)
    adder = jax.vmap(add_rows)

    def upper(field):
        return jnp.concatenate([field[1:], jnp.zeros_like(field[:1])], 0)

    def forward(field):
        spring_part = lax.optimization_barrier(jnp.sum(slopes * (picker(field, head_idx) - picker(field, tail_idx)), axis=1))
        corr_part = active * (picker(field, near_idx) - picker(upper(field), far_idx))
        return (spring_part, corr_part)

    def adjoint(spring_part, corr_part):
        zeros_field = jnp.zeros_like(positions)
        terms = slopes * spring_part[:, None, :]
        accum = adder(zeros_field, head_idx, terms)
        accum = adder(accum, tail_idx, -terms)
        accum = adder(accum, near_idx, active * corr_part)
        returned = adder(zeros_field, far_idx, -(active * corr_part))
        return accum + jnp.concatenate([jnp.zeros_like(returned[:1]), returned[:-1]], 0)

    def operator(field):
        spring_part, corr_part = forward(movable * field)
        return movable * adjoint(spring_part, corr_part) + DAMPING * field
    corr_res = active * (picker(positions, near_idx) - picker(upper(positions), far_idx))
    gradient = -movable * adjoint(spring_res, corr_res)
    solution_field = jnp.zeros_like(positions)
    residual = gradient
    search = gradient
    norm_now = jnp.sum(residual * residual)
    for turn in range(ITERS):
        image = operator(search)
        step_size = norm_now / jnp.sum(search * image)
        solution_field = solution_field + step_size * search
        residual = residual - step_size * image
        norm_next = jnp.sum(residual * residual)
        search = residual + norm_next / norm_now * search
        norm_now = norm_next
    return (solution_field, residual)
```

```python
import functools

import jax
import jax.numpy as jnp
from jax import lax
from jax.experimental import pallas as pl
from jax.experimental.pallas import tpu as pltpu
from jax.sharding import PartitionSpec as P

ITERS = 4
DAMPING = 0.05
LANES = 128
GROUP = 8
MESH = pl.DeviceIdType.MESH


def pick(line_of, parts, blocks):
    outs = [[jnp.zeros(lo.shape, jnp.float32) for _ in range(2)] for lo, _ in blocks]
    for h in range(parts):
        for c in range(2):
            line = line_of(c * parts + h)
            for k, (lo, hi) in enumerate(blocks):
                got = jnp.take_along_axis(
                    jnp.broadcast_to(line, lo.shape), lo, axis=1, mode="promise_in_bounds"
                )
                outs[k][c] = jnp.where(hi == h, got, outs[k][c])
    return outs


def split_index(index):
    return index & (LANES - 1), index >> 7


def kernel(
    count,
    corr_count, fixed, positions, edges, rest_length, stiffness, corr_index,
    solution_out, residual_out,
    index, rest, stiff, lo_hot, hi_hot, slope, spring, spring_old, corr_old, terms,
    table, next_table, far_here, far_prev, corr_send, corr_recv, sums, search,
    table_sems, corr_sems, sum_sems, far_sems,
):
    me = lax.axis_index("gz")
    has_next = me < count - 1
    has_prev = me > 0
    upper = {"gz": jnp.minimum(me + 1, count - 1)}
    lower = {"gz": jnp.maximum(me - 1, 0)}
    parts = positions.shape[2] // LANES
    springs = rest_length.shape[1] // LANES
    slots = corr_index.shape[2] // LANES
    groups = springs // GROUP
    wide = GROUP * LANES
    f32, bf16 = jnp.float32, jnp.bfloat16

    barrier = pltpu.get_barrier_semaphore()
    for step in range(1, count):
        other = lax.rem(me + step, count)
        pl.semaphore_signal(barrier, inc=1, device_id={"gz": other}, device_id_type=MESH)

    def lanes(k):
        return slice(k * LANES, (k + 1) * LANES)

    for s in range(slots):
        far_here[s : s + 1, :] = corr_index[0, 1:2, lanes(s)]
        index[2 * springs + s : 2 * springs + s + 1, :] = corr_index[0, 0:1, lanes(s)]
    for c in range(2):
        for h in range(parts):
            table[0, c * parts + h : c * parts + h + 1, :] = positions[0, c : c + 1, lanes(h)]
    for k in range(springs):
        index[k : k + 1, :] = edges[0, 0:1, lanes(k)]
        index[springs + k : springs + k + 1, :] = edges[0, 1:2, lanes(k)]
        rest[k : k + 1, :] = rest_length[0:1, lanes(k)]
        stiff[k : k + 1, :] = stiffness[0:1, lanes(k)]

    @pl.when(me == 0)
    def _():
        far_prev[...] = jnp.zeros_like(far_prev)
        corr_recv[...] = jnp.zeros_like(corr_recv)

    @pl.when(me == count - 1)
    def _():
        next_table[...] = jnp.zeros_like(next_table)

    search[...] = jnp.zeros_like(search)
    spring_old[...] = jnp.zeros_like(spring_old)
    corr_old[...] = jnp.zeros_like(corr_old)

    movable = (1 - fixed[0]).astype(f32)
    slot = (
        lax.broadcasted_iota(jnp.int32, (slots, LANES), 0) * LANES
        + lax.broadcasted_iota(jnp.int32, (slots, LANES), 1)
    )
    active = slot < corr_count[0]

    def table_copy(turn):
        return pltpu.make_async_remote_copy(
            src_ref=table.at[turn], dst_ref=next_table.at[turn],
            send_sem=table_sems.at[0, turn], recv_sem=table_sems.at[1, turn],
            device_id=lower, device_id_type=MESH,
        )

    def corr_copy(turn):
        return pltpu.make_async_remote_copy(
            src_ref=corr_send.at[turn], dst_ref=corr_recv.at[turn],
            send_sem=corr_sems.at[0, turn], recv_sem=corr_sems.at[1, turn],
            device_id=upper, device_id_type=MESH,
        )

    far_copy = pltpu.make_async_remote_copy(
        src_ref=far_here, dst_ref=far_prev,
        send_sem=far_sems.at[0], recv_sem=far_sems.at[1],
        device_id=upper, device_id_type=MESH,
    )

    def sum_start(place, value):
        sums[place, me] = jnp.sum(value, axis=0, keepdims=True)
        for step in range(1, count):
            pltpu.make_async_remote_copy(
                src_ref=sums.at[place, me], dst_ref=sums.at[place, me],
                send_sem=sum_sems.at[0, place], recv_sem=sum_sems.at[1, place],
                device_id={"gz": lax.rem(me + step, count)}, device_id_type=MESH,
            ).start()

    def sum_all(place):
        part = sums.at[place, pl.ds(0, count - 1)]
        return pltpu.make_async_remote_copy(
            src_ref=part, dst_ref=part,
            send_sem=sum_sems.at[0, place], recv_sem=sum_sems.at[1, place],
            device_id={"gz": lax.rem(me + 1, count)}, device_id_type=MESH,
        )

    def sum_finish(place):
        sum_all(place).wait_recv()
        return jnp.sum(jnp.sum(sums[place], axis=0), axis=1, keepdims=True)

    pl.semaphore_wait(barrier, count - 1)

    @pl.when(has_next)
    def _():
        far_copy.start()

    @pl.when(has_prev)
    def _():
        table_copy(0).start()

    def hot(line, chunk, sign):
        lo, hi = split_index(line)
        at = pl.ds(pl.multiple_of(chunk * LANES, LANES), LANES)
        rows = lax.broadcasted_iota(jnp.int32, (LANES, LANES), 0)
        lo_hot[:, at] = jnp.where(lo == rows, 1.0, 0.0).astype(bf16)
        rows = lax.broadcasted_iota(jnp.int32, (parts, LANES), 0)
        hi_hot[:, at] = jnp.where(hi == rows, sign, 0.0).astype(bf16)

    def hot_springs(k, _):
        hot(index[pl.ds(k, 1), :], k, 1.0)
        hot(index[pl.ds(springs + k, 1), :], springs + k, -1.0)
        return 0

    lax.fori_loop(0, springs, hot_springs, 0)
    for s in range(slots):
        hot(index[2 * springs + s : 2 * springs + s + 1, :], 2 * springs + s, 1.0)

    def rows_of(k):
        return pl.ds(pl.multiple_of(k * GROUP, GROUP), GROUP)

    def spread_of(turn, k):
        head = split_index(index[rows_of(k), :])
        tail = split_index(index[rows_of(k + groups), :])
        a, b = pick(lambda row: table[turn, row : row + 1, :], parts, [head, tail])
        return a[0] - b[0], a[1] - b[1]

    def corr_parts(turn):
        near = split_index(index[2 * springs : 2 * springs + slots, :])
        (a,) = pick(lambda row: table[turn, row : row + 1, :], parts, [near])

        @pl.when(has_next)
        def _():
            table_copy(turn).wait_recv()

        far = split_index(far_here[...])
        (b,) = pick(lambda row: next_table[turn, row : row + 1, :], parts, [far])
        return [jnp.where(active, a[c] - b[c], 0.0) for c in range(2)]

    def put_terms(c, rows, value):
        first = value.astype(bf16).astype(f32)
        terms[2 * c, rows, :] = first
        terms[2 * c + 1, rows, :] = value - first

    def spread_terms(row, lines):
        made = [[] for _ in lines]
        for i in range(GROUP):
            pieces = [[] for _ in lines]
            for part in range(4):
                value = jnp.broadcast_to(terms[part, pl.ds(row + i, 1), :], (parts, LANES)).astype(bf16)
                for piece, line in zip(pieces, lines):
                    at = pl.ds(pl.multiple_of((line + i) * LANES, LANES), LANES)
                    piece.append(value * hi_hot[:, at])
            for k, piece in enumerate(pieces):
                made[k].append(jnp.concatenate(piece, axis=0))
        return [jnp.concatenate(m, axis=1) for m in made]

    def add_terms(total, row, lines):
        for left, line in zip(spread_terms(row, lines), lines):
            right = lo_hot[:, pl.ds(pl.multiple_of(line * LANES, LANES), wide)]
            total += lax.dot_general(left, right, (((1,), (1,)), ((), ())), preferred_element_type=f32)
        return total

    def adjoint(turn, ready):
        def body(k, total):
            return add_terms(total, k * GROUP, (k * GROUP, springs + k * GROUP))

        total = lax.fori_loop(0, groups, body, jnp.zeros((4 * parts, LANES), f32))
        for s in range(0, slots, GROUP):
            total = add_terms(total, springs + s, (2 * springs + s,))
        ready()

        @pl.when(has_prev)
        def _():
            corr_copy(turn).wait_recv()

        for c in range(2):
            put_terms(c, pl.ds(springs + slots, slots), corr_recv[turn, c])
        for s in range(0, slots, GROUP):
            total = add_terms(total, springs + slots + s, (2 * springs + slots + s,))
        return jnp.concatenate(
            [total[2 * c * parts : (2 * c + 1) * parts] + total[(2 * c + 1) * parts : (2 * c + 2) * parts]
             for c in range(2)], axis=0,
        )

    def send_corr(turn, value):
        for c in range(2):
            corr_send[turn, c] = value[c]
            put_terms(c, pl.ds(springs, slots), value[c])

        @pl.when(has_next)
        def _():
            corr_copy(turn).start()

    def first_springs(k, _):
        dx, dy = spread_of(0, k)
        rows = rows_of(k)
        length = jnp.sqrt((dx * dx + dy * dy) + 1.0)
        part = stiff[rows, :] * (length - rest[rows, :])
        for c, d in enumerate((dx, dy)):
            value = stiff[rows, :] * d / length
            slope[c, rows, :] = value
            put_terms(c, rows, value * part)
        return 0

    lax.fori_loop(0, groups, first_springs, 0)
    send_corr(0, corr_parts(0))

    def far_ready():
        @pl.when(has_prev)
        def _():
            far_copy.wait_recv()

        for s in range(slots):
            hot(far_prev[s : s + 1, :], 2 * springs + slots + s, -1.0)

    residual_out[...] = -movable * adjoint(0, far_ready)
    solution_out[...] = jnp.zeros_like(solution_out)

    def folded(value):
        return jnp.sum(value.reshape(-1, 8, LANES), axis=0)

    def turn_body(turn, norm_before):
        place = 2 * (turn - 1)
        residual = residual_out[...]
        table[turn] = movable * residual

        @pl.when(has_prev)
        def _():
            table_copy(turn).start()

        sum_start(place, folded(residual * residual))

        def springs_body(k, _):
            dx, dy = spread_of(turn, k)
            rows = rows_of(k)
            spring[rows, :] = slope[0, rows, :] * dx + slope[1, rows, :] * dy
            return 0

        lax.fori_loop(0, groups, springs_body, 0)
        corr = corr_parts(turn)
        norm_now = sum_finish(place)
        ratio = jnp.where(turn == 1, 0.0, norm_now / norm_before)
        corr = [corr[c] + ratio * corr_old[c] for c in range(2)]
        for c in range(2):
            corr_old[c] = corr[c]
        send_corr(turn, corr)
        direction = residual_out[...] + ratio * search[...]
        search[...] = direction
        stretch = spring[...] + ratio * spring_old[...]
        spring_old[...] = stretch
        power = folded(stretch * stretch) + DAMPING * folded(direction * direction)
        power += folded(corr[0] * corr[0] + corr[1] * corr[1])
        sum_start(place + 1, power)
        for c in range(2):
            put_terms(c, pl.ds(0, springs), slope[c] * stretch)
        image = movable * adjoint(turn, lambda: None) + DAMPING * search[...]
        step_size = norm_now / sum_finish(place + 1)
        solution_out[...] += step_size * search[...]
        residual_out[...] -= step_size * image
        return norm_now

    lax.fori_loop(1, ITERS + 1, turn_body, jnp.ones((1, 1), f32))

    @pl.when(has_next)
    def _():
        far_copy.wait_send()
        for turn in range(ITERS + 1):
            corr_copy(turn).wait_send()

    @pl.when(has_prev)
    def _():
        for turn in range(ITERS + 1):
            table_copy(turn).wait_send()

    for place in range(2 * ITERS):
        sum_all(place).wait_send()


def shards(count, positions, edges, rest_length, stiffness, corr_index, corr_count, fixed):
    verts, slots = positions.shape[2] // LANES, corr_index.shape[2] // LANES
    springs = rest_length.shape[1] // LANES
    columns = 2 * (springs + slots) * LANES
    turns = ITERS + 1
    f32 = jnp.float32
    out = jax.ShapeDtypeStruct((2 * verts, LANES), f32)
    vmem, smem = pl.BlockSpec(memory_space=pltpu.VMEM), pl.BlockSpec(memory_space=pltpu.SMEM)
    answer, residual = pl.pallas_call(
        functools.partial(kernel, count),
        out_shape=(out, out),
        in_specs=[smem, smem, vmem, vmem, vmem, vmem, vmem],
        out_specs=(vmem, vmem),
        scratch_shapes=[
            pltpu.VMEM((2 * springs + slots, LANES), jnp.int32),
            pltpu.VMEM((springs, LANES), f32),
            pltpu.VMEM((springs, LANES), f32),
            pltpu.VMEM((LANES, columns), jnp.bfloat16),
            pltpu.VMEM((verts, columns), jnp.bfloat16),
            pltpu.VMEM((2, springs, LANES), f32),
            pltpu.VMEM((springs, LANES), f32),
            pltpu.VMEM((springs, LANES), f32),
            pltpu.VMEM((2, slots, LANES), f32),
            pltpu.VMEM((4, springs + 2 * slots, LANES), f32),
            pltpu.VMEM((turns, 2 * verts, LANES), f32),
            pltpu.VMEM((turns, 2 * verts, LANES), f32),
            pltpu.VMEM((slots, LANES), jnp.int32),
            pltpu.VMEM((slots, LANES), jnp.int32),
            pltpu.VMEM((turns, 2, slots, LANES), f32),
            pltpu.VMEM((turns, 2, slots, LANES), f32),
            pltpu.VMEM((2 * ITERS, count, 1, LANES), f32),
            pltpu.VMEM((2 * verts, LANES), f32),
            pltpu.SemaphoreType.DMA((2, turns)),
            pltpu.SemaphoreType.DMA((2, turns)),
            pltpu.SemaphoreType.DMA((2, 2 * ITERS)),
            pltpu.SemaphoreType.DMA((2,)),
        ],
        compiler_params=pltpu.CompilerParams(
            collective_id=0, has_side_effects=True, vmem_limit_bytes=40 * 2**20
        ),
        name="align",
    )(corr_count, fixed, positions, edges, rest_length, stiffness, corr_index)
    return answer.reshape(positions.shape), residual.reshape(positions.shape)


def solution(mesh):
    row = P(("groups", "gz"))
    return jax.shard_map(
        functools.partial(shards, mesh.shape["gz"]),
        mesh=mesh,
        in_specs=(row,) * 7,
        out_specs=(row, row),
        check_vma=False,
    )
```

```python
import functools

import jax
import jax.numpy as jnp
from jax import lax
from jax.experimental import pallas as pl
from jax.experimental.pallas import tpu as pltpu
from jax.sharding import PartitionSpec as P

ITERS = 4
DAMPING = 0.05
LANES = 128
GROUP = 8
GATHER_UNROLL = 8
SCATTER_UNROLL = 8
MESH = pl.DeviceIdType.MESH


def pick(line_of, parts, blocks):
    outs = [[jnp.zeros(lo.shape, jnp.float32) for _ in range(2)] for lo, _ in blocks]
    for h in range(parts):
        for c in range(2):
            line = line_of(c * parts + h)
            for k, (lo, hi) in enumerate(blocks):
                got = jnp.take_along_axis(
                    jnp.broadcast_to(line, lo.shape), lo, axis=1, mode="promise_in_bounds"
                )
                outs[k][c] = jnp.where(hi == h, got, outs[k][c])
    return outs


def split_index(index):
    return index & (LANES - 1), index >> 7


def kernel(
    count,
    corr_count, fixed, positions_in, edges_in, rest_in, stiffness_in, corr_index_in,
    solution_out, residual_out,
    positions, edges, rest_length, stiffness, corr_index,
    index, rest, stiff, lo_hot, hi_hot, slope, terms,
    table, next_table, prev_table, pair_here, pair_prev, sums, search, product, search_product, twice,
    lower_sems, upper_sems, sum_sems, pair_sems, in_sems,
):
    me = lax.axis_index("gz")
    has_next = me < count - 1
    has_prev = me > 0
    upper = {"gz": jnp.minimum(me + 1, count - 1)}
    lower = {"gz": jnp.maximum(me - 1, 0)}
    parts = positions.shape[2] // LANES
    springs = rest_length.shape[1] // LANES
    slots = corr_index.shape[2] // LANES
    groups = springs // GROUP
    wide = GROUP * LANES
    f32, bf16 = jnp.float32, jnp.bfloat16

    loads = [
        pltpu.make_async_copy(source, place, in_sems.at[k])
        for k, (source, place) in enumerate((
            (corr_index_in, corr_index), (positions_in, positions), (edges_in, edges),
            (rest_in, rest_length), (stiffness_in, stiffness),
        ))
    ]
    for load in loads:
        load.start()
    barrier = pltpu.get_barrier_semaphore()
    for step in range(1, count):
        other = lax.rem(me + step, count)
        pl.semaphore_signal(barrier, inc=1, device_id={"gz": other}, device_id_type=MESH)

    def lanes(k):
        return slice(k * LANES, (k + 1) * LANES)

    for load in loads:
        load.wait()
    for s in range(slots):
        slot = s * LANES + lax.broadcasted_iota(jnp.int32, (1, LANES), 1)
        for c in range(2):
            pair_here[c, s : s + 1, :] = jnp.where(slot < corr_count[0], corr_index[0, c : c + 1, lanes(s)], -1)
    for c in range(2):
        for h in range(parts):
            table[0, c * parts + h : c * parts + h + 1, :] = positions[0, c : c + 1, lanes(h)]
    for k in range(springs):
        index[k : k + 1, :] = edges[0, 0:1, lanes(k)]
        index[springs + k : springs + k + 1, :] = edges[0, 1:2, lanes(k)]
        rest[k : k + 1, :] = rest_length[0:1, lanes(k)]
        stiff[k : k + 1, :] = stiffness[0:1, lanes(k)]

    @pl.when(me == 0)
    def _():
        pair_prev[...] = jnp.full_like(pair_prev, -1)
        prev_table[...] = jnp.zeros_like(prev_table)

    @pl.when(me == count - 1)
    def _():
        next_table[...] = jnp.zeros_like(next_table)

    search[...] = jnp.zeros_like(search)
    search_product[...] = jnp.zeros_like(search_product)
    twice[...] = jnp.zeros_like(twice)

    movable = (1 - fixed[0]).astype(f32)
    def lower_copy(turn):
        return pltpu.make_async_remote_copy(
            src_ref=table.at[turn], dst_ref=next_table.at[turn],
            send_sem=lower_sems.at[0, turn], recv_sem=lower_sems.at[1, turn],
            device_id=lower, device_id_type=MESH,
        )

    def upper_copy(turn):
        return pltpu.make_async_remote_copy(
            src_ref=table.at[turn], dst_ref=prev_table.at[turn],
            send_sem=upper_sems.at[0, turn], recv_sem=upper_sems.at[1, turn],
            device_id=upper, device_id_type=MESH,
        )

    pair_copy = pltpu.make_async_remote_copy(
        src_ref=pair_here, dst_ref=pair_prev,
        send_sem=pair_sems.at[0], recv_sem=pair_sems.at[1],
        device_id=upper, device_id_type=MESH,
    )

    def table_start(turn):
        @pl.when(has_prev)
        def _():
            lower_copy(turn).start()

        @pl.when(has_next)
        def _():
            upper_copy(turn).start()

    def table_wait(turn):
        @pl.when(has_next)
        def _():
            lower_copy(turn).wait_recv()

        @pl.when(has_prev)
        def _():
            upper_copy(turn).wait_recv()

    def sum_start(place, value):
        sums[place, me] = value
        for step in range(1, count):
            pltpu.make_async_remote_copy(
                src_ref=sums.at[place, me], dst_ref=sums.at[place, me],
                send_sem=sum_sems.at[0, place], recv_sem=sum_sems.at[1, place],
                device_id={"gz": lax.rem(me + step, count)}, device_id_type=MESH,
            ).start()

    def sum_all(place):
        part = sums.at[place, pl.ds(0, count - 1)]
        return pltpu.make_async_remote_copy(
            src_ref=part, dst_ref=part,
            send_sem=sum_sems.at[0, place], recv_sem=sum_sems.at[1, place],
            device_id={"gz": lax.rem(me + 1, count)}, device_id_type=MESH,
        )

    def sum_finish(place):
        sum_all(place).wait_recv()
        return jnp.sum(sums[place], axis=0)

    pl.semaphore_wait(barrier, count - 1)

    @pl.when(has_next)
    def _():
        pair_copy.start()

    table_start(0)

    def hot(line, chunk, sign):
        lo, hi = split_index(line)
        at = pl.ds(pl.multiple_of(chunk * LANES, LANES), LANES)
        rows = lax.broadcasted_iota(jnp.int32, (LANES, LANES), 0)
        lo_hot[:, at] = jnp.where(lo == rows, 1.0, 0.0).astype(bf16)
        rows = lax.broadcasted_iota(jnp.int32, (parts, LANES), 0)
        hi_hot[:, at] = jnp.where(hi == rows, sign, 0.0).astype(bf16)

    def hot_springs(k, _):
        hot(index[pl.ds(k, 1), :], k, 1.0)
        hot(index[pl.ds(springs + k, 1), :], springs + k, -1.0)
        return 0

    lax.fori_loop(0, springs, hot_springs, 0)
    for s in range(slots):
        hot(pair_here[0, s : s + 1, :], 2 * springs + s, 1.0)

    def rows_of(k):
        return pl.ds(pl.multiple_of(k * GROUP, GROUP), GROUP)

    def spread_of(turn, k):
        head = split_index(index[rows_of(k), :])
        tail = split_index(index[rows_of(k + groups), :])
        a, b = pick(lambda row: table[turn, row : row + 1, :], parts, [head, tail])
        return a[0] - b[0], a[1] - b[1]

    def corr_terms(turn):
        own = lambda row: table[turn, row : row + 1, :]
        near, before = pick(own, parts, [split_index(pair_here[0]), split_index(pair_prev[1])])
        (far,) = pick(lambda row: next_table[turn, row : row + 1, :], parts, [split_index(pair_here[1])])
        (behind,) = pick(lambda row: prev_table[turn, row : row + 1, :], parts, [split_index(pair_prev[0])])
        for c in range(2):
            put_terms(c, pl.ds(springs, slots), near[c] - far[c])
            put_terms(c, pl.ds(springs + slots, slots), behind[c] - before[c])

    def put_terms(c, rows, value):
        first = value.astype(bf16).astype(f32)
        terms[2 * c, rows, :] = first
        terms[2 * c + 1, rows, :] = value - first

    def spread_terms(row, lines):
        made = [[] for _ in lines]
        for i in range(GROUP):
            pieces = [[] for _ in lines]
            for part in range(4):
                value = jnp.broadcast_to(terms[part, pl.ds(row + i, 1), :], (parts, LANES)).astype(bf16)
                for piece, line in zip(pieces, lines):
                    at = pl.ds(pl.multiple_of((line + i) * LANES, LANES), LANES)
                    piece.append(value * hi_hot[:, at])
            for k, piece in enumerate(pieces):
                made[k].append(jnp.concatenate(piece, axis=0))
        return [jnp.concatenate(m, axis=1) for m in made]

    def add_terms(total, row, lines):
        for left, line in zip(spread_terms(row, lines), lines):
            right = lo_hot[:, pl.ds(pl.multiple_of(line * LANES, LANES), wide)]
            total += lax.dot_general(left, right, (((1,), (1,)), ((), ())), preferred_element_type=f32)
        return total

    def adjoint(turn, ready):
        def body(k, total):
            return add_terms(total, k * GROUP, (k * GROUP, springs + k * GROUP))

        total = lax.fori_loop(0, groups, body, jnp.zeros((4 * parts, LANES), f32), unroll=SCATTER_UNROLL)
        table_wait(turn)
        ready()
        corr_terms(turn)
        for s in range(0, 2 * slots, GROUP):
            total = add_terms(total, springs + s, (2 * springs + s,))
        return jnp.concatenate(
            [total[2 * c * parts : (2 * c + 1) * parts] + total[(2 * c + 1) * parts : (2 * c + 2) * parts]
             for c in range(2)], axis=0,
        )

    def first_springs(k, _):
        dx, dy = spread_of(0, k)
        rows = rows_of(k)
        length = jnp.sqrt((dx * dx + dy * dy) + 1.0)
        part = stiff[rows, :] * (length - rest[rows, :])
        for c, d in enumerate((dx, dy)):
            value = stiff[rows, :] * d / length
            slope[c, rows, :] = value
            put_terms(c, rows, value * part)
        return 0

    lax.fori_loop(0, groups, first_springs, 0, unroll=GATHER_UNROLL)

    def far_ready():
        @pl.when(has_prev)
        def _():
            pair_copy.wait_recv()

        for s in range(slots):
            hot(pair_prev[1, s : s + 1, :], 2 * springs + slots + s, -1.0)

    residual_out[...] = -movable * adjoint(0, far_ready)
    solution_out[...] = jnp.zeros_like(solution_out)

    def folded(value):
        return jnp.sum(value.reshape(-1, 8, LANES), axis=0)

    def matvec(turn, vector):
        def springs_body(k, _):
            dx, dy = spread_of(turn, k)
            rows = rows_of(k)
            part = slope[0, rows, :] * dx + slope[1, rows, :] * dy
            for c in range(2):
                put_terms(c, rows, slope[c, rows, :] * part)
            return 0

        lax.fori_loop(0, groups, springs_body, 0, unroll=GATHER_UNROLL)
        return movable * adjoint(turn, lambda: None) + DAMPING * vector[...]

    product[...] = residual_out[...]
    lane = lax.broadcasted_iota(jnp.int32, (1, LANES), 1)

    def turn_body(turn, before):
        norm_before, power_before = before
        if turn_copies(turn):
            table[turn] = movable * product[...]
            table_start(turn)

        residual = residual_out[...]
        dots = jnp.concatenate([
            jnp.sum(folded(residual * other), axis=0, keepdims=True)
            for other in (residual, product[...], search_product[...])
        ], axis=0)
        dots = jnp.sum(dots, axis=1, keepdims=True)
        sum_start(turn - 1, sum(jnp.where(lane == k, dots[k : k + 1], 0.0) for k in range(3)))
        image = matvec(turn, product) if turn_copies(turn) else None
        dots = sum_finish(turn - 1)
        norm, cross, mixed = (dots[:, k : k + 1] for k in range(3))
        live = turn > 1
        ratio = jnp.where(turn > 2, norm / norm_before, 0.0)
        power = cross + ratio * (2.0 * mixed + ratio * power_before)
        step_size = jnp.where(live, norm / power, 0.0)
        direction = residual_out[...] + ratio * search[...]
        moved = product[...] + ratio * search_product[...]
        search[...] = direction
        search_product[...] = moved
        solution_out[...] += step_size * direction
        residual_out[...] -= step_size * moved
        if image is not None:
            again = image + ratio * twice[...]
            twice[...] = again
            product[...] = jnp.where(live, product[...] - step_size * again, image)
        return norm, power

    def turn_copies(turn):
        return not isinstance(turn, int)

    ones = jnp.ones((1, 1), f32)
    last = lax.fori_loop(1, ITERS + 1, turn_body, (ones, ones))
    turn_body(ITERS + 1, last)

    @pl.when(has_next)
    def _():
        pair_copy.wait_send()
        for turn in range(ITERS + 1):
            upper_copy(turn).wait_send()

    @pl.when(has_prev)
    def _():
        for turn in range(ITERS + 1):
            lower_copy(turn).wait_send()

    for place in range(ITERS + 1):
        sum_all(place).wait_send()


def shards(count, positions, edges, rest_length, stiffness, corr_index, corr_count, fixed):
    verts, slots = positions.shape[2] // LANES, corr_index.shape[2] // LANES
    springs = rest_length.shape[1] // LANES
    columns = 2 * (springs + slots) * LANES
    turns = ITERS + 1
    f32 = jnp.float32
    out = jax.ShapeDtypeStruct((2 * verts, LANES), f32)
    vmem, smem = pl.BlockSpec(memory_space=pltpu.VMEM), pl.BlockSpec(memory_space=pltpu.SMEM)
    answer, residual = pl.pallas_call(
        functools.partial(kernel, count),
        out_shape=(out, out),
        in_specs=[smem, smem] + [pl.BlockSpec(memory_space=pltpu.HBM)] * 5,
        out_specs=(vmem, vmem),
        scratch_shapes=[
            pltpu.VMEM(positions.shape, f32),
            pltpu.VMEM(edges.shape, jnp.int32),
            pltpu.VMEM(rest_length.shape, f32),
            pltpu.VMEM(stiffness.shape, f32),
            pltpu.VMEM(corr_index.shape, jnp.int32),
            pltpu.VMEM((2 * springs, LANES), jnp.int32),
            pltpu.VMEM((springs, LANES), f32),
            pltpu.VMEM((springs, LANES), f32),
            pltpu.VMEM((LANES, columns), jnp.bfloat16),
            pltpu.VMEM((verts, columns), jnp.bfloat16),
            pltpu.VMEM((2, springs, LANES), f32),
            pltpu.VMEM((4, springs + 2 * slots, LANES), f32),
            pltpu.VMEM((turns, 2 * verts, LANES), f32),
            pltpu.VMEM((turns, 2 * verts, LANES), f32),
            pltpu.VMEM((turns, 2 * verts, LANES), f32),
            pltpu.VMEM((2, slots, LANES), jnp.int32),
            pltpu.VMEM((2, slots, LANES), jnp.int32),
            pltpu.VMEM((turns, count, 1, LANES), f32),
            pltpu.VMEM((2 * verts, LANES), f32),
            pltpu.VMEM((2 * verts, LANES), f32),
            pltpu.VMEM((2 * verts, LANES), f32),
            pltpu.VMEM((2 * verts, LANES), f32),
            pltpu.SemaphoreType.DMA((2, turns)),
            pltpu.SemaphoreType.DMA((2, turns)),
            pltpu.SemaphoreType.DMA((2, turns)),
            pltpu.SemaphoreType.DMA((2,)),
            pltpu.SemaphoreType.DMA((5,)),
        ],
        compiler_params=pltpu.CompilerParams(
            collective_id=0, has_side_effects=True, vmem_limit_bytes=40 * 2**20
        ),
        name="align",
    )(corr_count, fixed, positions, edges, rest_length, stiffness, corr_index)
    return answer.reshape(positions.shape), residual.reshape(positions.shape)


def solution(mesh):
    row = P(("groups", "gz"))
    return jax.shard_map(
        functools.partial(shards, mesh.shape["gz"]),
        mesh=mesh,
        in_specs=(row,) * 7,
        out_specs=(row, row),
        check_vma=False,
    )
```

```python
import functools

import jax
import jax.numpy as jnp
from jax import lax
from jax.experimental import pallas as pl
from jax.experimental.pallas import tpu as pltpu
from jax.sharding import PartitionSpec as P

ITERS = 4
DAMPING = 0.05
LANES = 128
GROUP = 8
SPLITS = 3
GATHER_UNROLL = 8
SCATTER_UNROLL = 8
MESH = pl.DeviceIdType.MESH


def pick(line_of, parts, blocks):
    outs = [[jnp.zeros(lo.shape, jnp.float32) for _ in range(2)] for lo, _ in blocks]
    for h in range(parts):
        for c in range(2):
            line = line_of(c * parts + h)
            for k, (lo, hi) in enumerate(blocks):
                got = jnp.take_along_axis(
                    jnp.broadcast_to(line, lo.shape), lo, axis=1, mode="promise_in_bounds"
                )
                outs[k][c] = jnp.where(hi == h, got, outs[k][c])
    return outs


def split_index(index):
    return index & (LANES - 1), index >> 7


def kernel(
    count,
    corr_count, fixed, positions_in, edges_in, rest_in, stiffness_in, corr_index_in,
    solution_out, residual_out,
    positions, edges, rest_length, stiffness, corr_index,
    index, rest, stiff, lo_hot, hi_hot, slope, terms,
    table, next_table, prev_table, pair_here, pair_prev, sums, sums_now, search, product, search_product, twice,
    lower_sems, upper_sems, sum_sems, pair_sems, in_sems,
):
    me = lax.axis_index("gz")
    has_next = me < count - 1
    has_prev = me > 0
    upper = {"gz": jnp.minimum(me + 1, count - 1)}
    lower = {"gz": jnp.maximum(me - 1, 0)}
    parts = positions.shape[2] // LANES
    springs = rest_length.shape[1] // LANES
    slots = corr_index.shape[2] // LANES
    groups = springs // GROUP
    wide = GROUP * LANES
    f32, bf16 = jnp.float32, jnp.bfloat16

    loads = [
        pltpu.make_async_copy(source, place, in_sems.at[k])
        for k, (source, place) in enumerate((
            (corr_index_in, corr_index), (positions_in, positions), (edges_in, edges),
            (rest_in, rest_length), (stiffness_in, stiffness),
        ))
    ]
    for load in loads:
        load.start()
    barrier = pltpu.get_barrier_semaphore()
    for step in range(1, count):
        other = lax.rem(me + step, count)
        pl.semaphore_signal(barrier, inc=1, device_id={"gz": other}, device_id_type=MESH)

    def lanes(k):
        return slice(k * LANES, (k + 1) * LANES)

    for load in loads:
        load.wait()
    for s in range(slots):
        slot = s * LANES + lax.broadcasted_iota(jnp.int32, (1, LANES), 1)
        for c in range(2):
            pair_here[c, s : s + 1, :] = jnp.where(slot < corr_count[0], corr_index[0, c : c + 1, lanes(s)], -1)
    for c in range(2):
        for h in range(parts):
            table[0, c * parts + h : c * parts + h + 1, :] = positions[0, c : c + 1, lanes(h)]
    for k in range(springs):
        index[k : k + 1, :] = edges[0, 0:1, lanes(k)]
        index[springs + k : springs + k + 1, :] = edges[0, 1:2, lanes(k)]
        rest[k : k + 1, :] = rest_length[0:1, lanes(k)]
        stiff[k : k + 1, :] = stiffness[0:1, lanes(k)]

    @pl.when(me == 0)
    def _():
        pair_prev[...] = jnp.full_like(pair_prev, -1)
        prev_table[...] = jnp.zeros_like(prev_table)

    @pl.when(me == count - 1)
    def _():
        next_table[...] = jnp.zeros_like(next_table)

    search[...] = jnp.zeros_like(search)
    search_product[...] = jnp.zeros_like(search_product)
    twice[...] = jnp.zeros_like(twice)

    movable = (1 - fixed[0]).astype(f32)
    def lower_copy(turn):
        return pltpu.make_async_remote_copy(
            src_ref=table.at[turn], dst_ref=next_table.at[turn],
            send_sem=lower_sems.at[0, turn], recv_sem=lower_sems.at[1, turn],
            device_id=lower, device_id_type=MESH,
        )

    def upper_copy(turn):
        return pltpu.make_async_remote_copy(
            src_ref=table.at[turn], dst_ref=prev_table.at[turn],
            send_sem=upper_sems.at[0, turn], recv_sem=upper_sems.at[1, turn],
            device_id=upper, device_id_type=MESH,
        )

    pair_copy = pltpu.make_async_remote_copy(
        src_ref=pair_here, dst_ref=pair_prev,
        send_sem=pair_sems.at[0], recv_sem=pair_sems.at[1],
        device_id=upper, device_id_type=MESH,
    )

    def table_start(turn):
        @pl.when(has_prev)
        def _():
            lower_copy(turn).start()

        @pl.when(has_next)
        def _():
            upper_copy(turn).start()

    def table_wait(turn):
        @pl.when(has_next)
        def _():
            lower_copy(turn).wait_recv()

        @pl.when(has_prev)
        def _():
            upper_copy(turn).wait_recv()

    def sum_start(place, value):
        sums[place, me] = value
        for step in range(1, count):
            pltpu.make_async_remote_copy(
                src_ref=sums.at[place, me], dst_ref=sums.at[place, me],
                send_sem=sum_sems.at[0, place], recv_sem=sum_sems.at[1, place],
                device_id={"gz": lax.rem(me + step, count)}, device_id_type=MESH,
            ).start()

    def sum_all(place):
        part = sums.at[place, pl.ds(0, count - 1)]
        return pltpu.make_async_remote_copy(
            src_ref=part, dst_ref=part,
            send_sem=sum_sems.at[0, place], recv_sem=sum_sems.at[1, place],
            device_id={"gz": lax.rem(me + 1, count)}, device_id_type=MESH,
        )

    def sum_finish(place):
        sum_all(place).wait_recv()
        return jnp.sum(sums[place], axis=0)

    pl.semaphore_wait(barrier, count - 1)

    @pl.when(has_next)
    def _():
        pair_copy.start()

    table_start(0)

    def hot(line, chunk, sign):
        lo, hi = split_index(line)
        at = pl.ds(pl.multiple_of(chunk * LANES, LANES), LANES)
        rows = lax.broadcasted_iota(jnp.int32, (LANES, LANES), 0)
        lo_hot[:, at] = jnp.where(lo == rows, 1.0, 0.0).astype(bf16)
        rows = lax.broadcasted_iota(jnp.int32, (parts, LANES), 0)
        hi_hot[:, at] = jnp.where(hi == rows, sign, 0.0).astype(bf16)

    def hot_springs(k, _):
        hot(index[pl.ds(k, 1), :], k, 1.0)
        hot(index[pl.ds(springs + k, 1), :], springs + k, -1.0)
        return 0

    lax.fori_loop(0, springs, hot_springs, 0)
    for s in range(slots):
        hot(pair_here[0, s : s + 1, :], 2 * springs + s, 1.0)

    def rows_of(k):
        return pl.ds(pl.multiple_of(k * GROUP, GROUP), GROUP)

    def spread_of(turn, k):
        head = split_index(index[rows_of(k), :])
        tail = split_index(index[rows_of(k + groups), :])
        a, b = pick(lambda row: table[turn, row : row + 1, :], parts, [head, tail])
        return a[0] - b[0], a[1] - b[1]

    def corr_terms(turn):
        own = lambda row: table[turn, row : row + 1, :]
        near, before = pick(own, parts, [split_index(pair_here[0]), split_index(pair_prev[1])])
        (far,) = pick(lambda row: next_table[turn, row : row + 1, :], parts, [split_index(pair_here[1])])
        (behind,) = pick(lambda row: prev_table[turn, row : row + 1, :], parts, [split_index(pair_prev[0])])
        for c in range(2):
            put_terms(c, pl.ds(springs, slots), near[c] - far[c])
            put_terms(c, pl.ds(springs + slots, slots), behind[c] - before[c])

    def put_terms(c, rows, value):
        for k in range(SPLITS):
            piece = value if k == SPLITS - 1 else value.astype(bf16).astype(f32)
            terms[SPLITS * c + k, rows, :] = piece
            value = value - piece

    def spread_terms(row, lines):
        made = [[] for _ in lines]
        for i in range(GROUP):
            pieces = [[] for _ in lines]
            for part in range(2 * SPLITS):
                value = jnp.broadcast_to(terms[part, pl.ds(row + i, 1), :], (parts, LANES)).astype(bf16)
                for piece, line in zip(pieces, lines):
                    at = pl.ds(pl.multiple_of((line + i) * LANES, LANES), LANES)
                    piece.append(value * hi_hot[:, at])
            for k, piece in enumerate(pieces):
                made[k].append(jnp.concatenate(piece, axis=0))
        return [jnp.concatenate(m, axis=1) for m in made]

    def add_terms(total, row, lines):
        for left, line in zip(spread_terms(row, lines), lines):
            right = lo_hot[:, pl.ds(pl.multiple_of(line * LANES, LANES), wide)]
            total += lax.dot_general(left, right, (((1,), (1,)), ((), ())), preferred_element_type=f32)
        return total

    def adjoint(turn, ready):
        def body(k, total):
            return add_terms(total, k * GROUP, (k * GROUP, springs + k * GROUP))

        total = lax.fori_loop(0, groups, body, jnp.zeros((2 * SPLITS * parts, LANES), f32), unroll=SCATTER_UNROLL)
        table_wait(turn)
        ready()
        corr_terms(turn)
        for s in range(0, 2 * slots, GROUP):
            total = add_terms(total, springs + s, (2 * springs + s,))
        total = total.reshape(2, SPLITS, parts, LANES)
        return jnp.concatenate([sum(total[c, k] for k in range(SPLITS)) for c in range(2)], axis=0)

    def first_springs(k, _):
        dx, dy = spread_of(0, k)
        rows = rows_of(k)
        length = jnp.sqrt((dx * dx + dy * dy) + 1.0)
        part = stiff[rows, :] * (length - rest[rows, :])
        for c, d in enumerate((dx, dy)):
            value = stiff[rows, :] * d / length
            slope[c, rows, :] = value
            put_terms(c, rows, value * part)
        return 0

    lax.fori_loop(0, groups, first_springs, 0, unroll=GATHER_UNROLL)

    def far_ready():
        @pl.when(has_prev)
        def _():
            pair_copy.wait_recv()

        for s in range(slots):
            hot(pair_prev[1, s : s + 1, :], 2 * springs + slots + s, -1.0)

    residual_out[...] = -movable * adjoint(0, far_ready)
    solution_out[...] = jnp.zeros_like(solution_out)

    def folded(value):
        return jnp.sum(value.reshape(-1, 8, LANES), axis=0)

    def matvec(turn, vector):
        def springs_body(k, _):
            dx, dy = spread_of(turn, k)
            rows = rows_of(k)
            part = slope[0, rows, :] * dx + slope[1, rows, :] * dy
            for c in range(2):
                put_terms(c, rows, slope[c, rows, :] * part)
            return 0

        lax.fori_loop(0, groups, springs_body, 0, unroll=GATHER_UNROLL)
        return movable * adjoint(turn, lambda: None) + DAMPING * vector[...]

    product[...] = residual_out[...]
    sums_now[...] = jnp.zeros_like(sums_now)
    lane = lax.broadcasted_iota(jnp.int32, (1, LANES), 1)

    def turn_body(turn, before):
        norm_before, power_before = before
        residual = residual_out[...]
        dots = jnp.concatenate([
            jnp.sum(folded(residual * other), axis=0, keepdims=True)
            for other in (residual, product[...], search_product[...])
        ], axis=0)
        dots = jnp.sum(dots, axis=1, keepdims=True)
        row = sum(jnp.where(lane == k, dots[k : k + 1], 0.0) for k in range(3))

        @pl.when(turn > 1)
        def _():
            sum_start(turn - 2, row)

        if turn_copies(turn):
            table[turn] = movable * product[...]
            table_start(turn)
        image = matvec(turn, product) if turn_copies(turn) else None

        @pl.when(turn > 1)
        def _():
            sums_now[...] = sum_finish(turn - 2)

        dots = sums_now[...]
        norm, cross, mixed = (dots[:, k : k + 1] for k in range(3))
        live = turn > 1
        ratio = jnp.where(turn > 2, norm / norm_before, 0.0)
        power = cross + ratio * (2.0 * mixed + ratio * power_before)
        step_size = jnp.where(live, norm / power, 0.0)
        direction = residual_out[...] + ratio * search[...]
        moved = product[...] + ratio * search_product[...]
        search[...] = direction
        search_product[...] = moved
        solution_out[...] += step_size * direction
        residual_out[...] -= step_size * moved
        if image is not None:
            again = image + ratio * twice[...]
            twice[...] = again
            product[...] = jnp.where(live, product[...] - step_size * again, image)
        return norm, power

    def turn_copies(turn):
        return not isinstance(turn, int)

    ones = jnp.ones((1, 1), f32)
    last = lax.fori_loop(1, ITERS + 1, turn_body, (ones, ones))
    turn_body(ITERS + 1, last)

    @pl.when(has_next)
    def _():
        pair_copy.wait_send()
        for turn in range(ITERS + 1):
            upper_copy(turn).wait_send()

    @pl.when(has_prev)
    def _():
        for turn in range(ITERS + 1):
            lower_copy(turn).wait_send()

    for place in range(ITERS):
        sum_all(place).wait_send()


def shards(count, positions, edges, rest_length, stiffness, corr_index, corr_count, fixed):
    verts, slots = positions.shape[2] // LANES, corr_index.shape[2] // LANES
    springs = rest_length.shape[1] // LANES
    columns = 2 * (springs + slots) * LANES
    turns = ITERS + 1
    f32 = jnp.float32
    out = jax.ShapeDtypeStruct((2 * verts, LANES), f32)
    vmem, smem = pl.BlockSpec(memory_space=pltpu.VMEM), pl.BlockSpec(memory_space=pltpu.SMEM)
    answer, residual = pl.pallas_call(
        functools.partial(kernel, count),
        out_shape=(out, out),
        in_specs=[smem, smem] + [pl.BlockSpec(memory_space=pltpu.HBM)] * 5,
        out_specs=(vmem, vmem),
        scratch_shapes=[
            pltpu.VMEM(positions.shape, f32),
            pltpu.VMEM(edges.shape, jnp.int32),
            pltpu.VMEM(rest_length.shape, f32),
            pltpu.VMEM(stiffness.shape, f32),
            pltpu.VMEM(corr_index.shape, jnp.int32),
            pltpu.VMEM((2 * springs, LANES), jnp.int32),
            pltpu.VMEM((springs, LANES), f32),
            pltpu.VMEM((springs, LANES), f32),
            pltpu.VMEM((LANES, columns), jnp.bfloat16),
            pltpu.VMEM((verts, columns), jnp.bfloat16),
            pltpu.VMEM((2, springs, LANES), f32),
            pltpu.VMEM((2 * SPLITS, springs + 2 * slots, LANES), f32),
            pltpu.VMEM((turns, 2 * verts, LANES), f32),
            pltpu.VMEM((turns, 2 * verts, LANES), f32),
            pltpu.VMEM((turns, 2 * verts, LANES), f32),
            pltpu.VMEM((2, slots, LANES), jnp.int32),
            pltpu.VMEM((2, slots, LANES), jnp.int32),
            pltpu.VMEM((ITERS, count, 1, LANES), f32),
            pltpu.VMEM((1, LANES), f32),
            pltpu.VMEM((2 * verts, LANES), f32),
            pltpu.VMEM((2 * verts, LANES), f32),
            pltpu.VMEM((2 * verts, LANES), f32),
            pltpu.VMEM((2 * verts, LANES), f32),
            pltpu.SemaphoreType.DMA((2, turns)),
            pltpu.SemaphoreType.DMA((2, turns)),
            pltpu.SemaphoreType.DMA((2, turns)),
            pltpu.SemaphoreType.DMA((2,)),
            pltpu.SemaphoreType.DMA((5,)),
        ],
        compiler_params=pltpu.CompilerParams(
            collective_id=0, has_side_effects=True, vmem_limit_bytes=40 * 2**20
        ),
        name="align",
    )(corr_count, fixed, positions, edges, rest_length, stiffness, corr_index)
    return answer.reshape(positions.shape), residual.reshape(positions.shape)


def solution(mesh):
    row = P(("groups", "gz"))
    return jax.shard_map(
        functools.partial(shards, mesh.shape["gz"]),
        mesh=mesh,
        in_specs=(row,) * 7,
        out_specs=(row, row),
        check_vma=False,
    )
```
